512 devices in a mesh: ry: 32 (over z, y_hi), rx: 16 (over y_lo, x, core).
Axes of the slice: x: 4, y: 4 (y_hi: 2, y_lo: 2; y = y_hi * 2 + y_lo), z: 16, core: 2. Of those that a mesh axis runs over, the one named last changes fastest.
Arguments:
- control: bfloat16 [2, 64, 256, 2048], P(None, None, 'ry', 'rx'), may hold values from -6 to 6
- forcing: bfloat16 [2, 64, 256, 2048], P(None, None, 'ry', 'rx'), may hold values from -0.1796875 to 0.1796875
- obs_tile: int32 [524288, 1], P(('ry', 'rx')), may hold values from 0 to 15; in each aligned block of 1024 rows (0 to 1023, 1024 to 2047, ...) at most 256 rows name the same one
- obs_cell: int32 [524288], P(('ry', 'rx')), may hold values from 0 to 65535
- obs_value: float32 [2, 524288], P(None, ('ry', 'rx')), may hold values from -6 to 6
- obs_count: int32 [512], P(('ry', 'rx')), may hold values from 256 to 1024, as said below
- rate_x: float32 [2048], replicated, may hold values from 0.5 to 8
- rate_y: float32 [256], P('ry'), may hold values from 0.5 to 8
- vert: bfloat16 [2, 64, 64], replicated, may hold values from -0.75 to 0.75
Outputs:
- gradient: bfloat16 [2, 64, 256, 2048], P(None, None, 'ry', 'rx')
The draws below stay inside these ranges and needn't reach their ends.
Inputs may be any that keep to these rules, and one draw needn't show every extreme that they name: `obs_tile`: among the 1024 slots of one region no tile is named more than 256 times; in some region some tile is named exactly 256 times. `obs_count`: some region uses all 1024 slots.
All inputs are finite; a program needn't handle non-finite values.
Results may differ from the reference program's by a relative error of at most 0.0067.
Values may be sent and summed in bfloat16 or wider, within the bound.
No kernel may reach another device: no remote copies, remote signals or barrier semaphores. Data moves between devices by JAX's collectives and lax.ppermute only.
A program may use at most 192 MiB of HBM per device.

```python
import math
import jax
import jax.numpy as jnp
import numpy as np
from jax import lax

C = 2
LEV = 64
CY = 8
CX = 128
OBS_DEV = 1024
HX = 128
HY = 8
NY = 256
NX = 2048
REGIONS = 512
NOBS = 524288
CAP = 256
N_RY = 32
N_RX = 16


def draw_obs_count(key, part):
    key = jax.random.fold_in(key, 7)
    first_key, second_key = jax.random.split(key)
    halvings = jax.random.randint(first_key, (REGIONS,), 0, 3)
    counts = OBS_DEV // jnp.power(2, halvings)
    full_region = jax.random.randint(second_key, (), 0, REGIONS)
    counts = jnp.where(jnp.arange(REGIONS) == full_region, OBS_DEV, counts)
    return counts.astype(jnp.int32)


def plant(drawn, own_key, smallest, largest):
    spot = [jax.random.randint(jax.random.fold_in(own_key, axis), (), 0, length) for axis, length in enumerate(drawn.shape)]
    widest = drawn.shape.index(max(drawn.shape))
    neighbour = spot[:widest] + [(spot[widest] + 1) % drawn.shape[widest]] + spot[widest + 1:]
    return drawn.at[tuple(spot)].set(smallest).at[tuple(neighbour)].set(largest)


def shard_levels(stream_key, shape, cuts, least, top_value):
    gain, own = 1.0, jax.random.fold_in(stream_key, 6)
    for axis_at, blocks in cuts:
        heights = jnp.exp(jax.random.uniform(jax.random.fold_in(own, axis_at), (blocks,), jnp.float32, least / len(cuts), top_value / len(cuts)))
        gain = gain * jnp.repeat(heights, shape[axis_at] // blocks).reshape([-1 if axis == axis_at else 1 for axis in range(len(shape))])
    return gain


def deal_out(stream_key, own, number, rows, amount, top, limit, skew):
    order = jax.random.permutation(stream_key, amount)
    crowded, ordinary = shares(amount, rows * top, limit, skew, True), shares(amount, rows * top, limit, skew, False)
    places = jnp.arange(amount)

    def named(tallies, offset_by):
        used = int((tallies > 0).sum())
        fixed = max(1, used // 4)
        passed = fixed + (places - fixed + offset_by * (used - fixed)) % max(1, amount - fixed)
        return jnp.zeros((amount,), jnp.int32).at[order[jnp.where(places < fixed, places, passed)]].set(jnp.asarray(tallies, jnp.int32))

    tallies = jnp.where(number % 4 == 0, named(crowded, number // 4), named(ordinary, number - number // 4 - 1))
    mixed = jax.random.permutation(jax.random.fold_in(own, 3), amount)
    source_of, receiver = mixed[0:amount // 2 * 2:2], mixed[1:amount // 2 * 2:2]
    slack = jnp.minimum(tallies[source_of] - 1, limit - tallies[receiver]) // 2
    slack = jnp.where((source_of == order[0]) | (receiver == order[0]) | (tallies[receiver] == 0), 0, jnp.maximum(slack, 0))
    passed = jax.random.randint(jax.random.fold_in(own, 4), (amount // 2,), 0, 1 << 20) % (slack + 1)
    tallies = tallies.at[source_of].add(-passed).at[receiver].add(passed)
    items = jnp.searchsorted(jnp.cumsum(tallies), jnp.arange(rows * top), side="right").astype(jnp.int32)
    table = items.reshape(top, rows).T
    table = table[jax.random.permutation(jax.random.fold_in(own, 1), rows)]
    offset_by = jax.random.randint(jax.random.fold_in(own, 2), (rows, 1), 0, top)
    return jnp.take_along_axis(table, (jnp.arange(top)[None, :] + offset_by) % top, axis=1)


def shares(number_of, total, limit, lean, full):
    portions = [(1 << 20) // math.isqrt(rank ** lean) + 1 for rank in range(1, number_of + 1)]
    largest = limit if full else min(limit, max(-(-total // number_of), total * portions[0] // sum(portions)))
    least = 1 if total - largest >= number_of - 1 else 0
    given, rest = [largest] + [least] * (number_of - 1), total - largest - least * (number_of - 1)
    while rest > 0:
        free = [i for i in range(1, number_of) if given[i] < largest] or [i for i in range(1, number_of) if given[i] < limit]
        whole, budget = sum([portions[i] for i in free]), rest
        for i in free:
            addition = min(limit - given[i], max(1, budget * portions[i] // whole), rest)
            given[i] = given[i] + addition
            rest = rest - addition
    return np.array(given)


def bell_draw(stream_key, shape, deviation, most, cuts=(), held_as=jnp.bfloat16):
    entries = deviation * jax.random.normal(stream_key, shape, jnp.float32)
    if cuts:
        entries = entries * shard_levels(stream_key, shape, cuts, -0.22, 0.18)
    return jnp.clip(entries, -most, most).astype(held_as)


def setup_inputs(seed: int = 0) -> dict:
    keys = jax.random.split(jax.random.key(seed), 10)
    control = bell_draw(keys[0], (C, LEV, NY, NX), 1.0, 6.0, ((2, 32), (3, 16)))
    forcing = bell_draw(keys[1], (C, LEV, NY, NX), 0.03, 0.1796875, ((2, 32), (3, 16)))
    obs_tile_keys = jax.random.split(jax.random.fold_in(keys[2], 1), NOBS // OBS_DEV)
    obs_tile_turns = jax.random.permutation(jax.random.fold_in(keys[2], 3), NOBS // OBS_DEV)
    obs_tile = jax.vmap(lambda own, number: deal_out(jax.random.fold_in(keys[2], 2), own, number, OBS_DEV, N_RX, 1, CAP, 2))(obs_tile_keys, obs_tile_turns).reshape((NOBS, 1))
    obs_cell = plant(jax.random.randint(keys[3], (NOBS,), 0, LEV * CY * CX), jax.random.fold_in(keys[3], 1), 0, (LEV * CY * CX) - 1).astype(jnp.int32)
    obs_value = bell_draw(keys[4], (C, NOBS), 1.0, 6.0, ((1, 512),), jnp.float32)
    obs_count = draw_obs_count(jax.random.fold_in(keys[9], 71), 0)
    rate_x = jnp.clip(jnp.exp(jax.random.uniform(keys[6], (NX,), jnp.float32, math.log(0.5), math.log(8.0))), 0.5, 8.0)
    rate_y = jnp.clip(jnp.exp(math.log(8.0) - 2.7725887 * jax.random.uniform(keys[7], (NY,), jnp.float32) ** shard_levels(keys[7], (NY,), ((0, 32),), -0.2, 0.2)), 0.5, 8.0)
    vert = bell_draw(keys[8], (C, LEV, LEV), LEV ** -0.5, 0.75)
    return dict(control=control, forcing=forcing, obs_tile=obs_tile, obs_cell=obs_cell, obs_value=obs_value, obs_count=obs_count, rate_x=rate_x, rate_y=rate_y, vert=vert)


def band_kernel(rates, reach_cells):
    block_count = rates.shape[0] // reach_cells
    offsets = jnp.arange(3)[:, None, None, None]
    in_cell = jnp.arange(reach_cells)[None, None, :, None]
    out_cell = jnp.arange(reach_cells)[None, None, None, :]
    distance = jnp.abs((offsets - 1) * reach_cells + in_cell - out_cell).astype(jnp.float32)
    scaled = rates.reshape(1, block_count, 1, reach_cells)
    weight = jnp.where(distance <= reach_cells, jnp.exp(-distance * scaled / reach_cells), 0.0)
    return weight.astype(jnp.bfloat16)


def lat_kernel(rates, reach_cells):
    row_count = rates.shape[0]
    out_row = jnp.arange(row_count)[:, None]
    in_row = jnp.arange(row_count + 2 * reach_cells)[None, :]
    distance = jnp.abs(in_row - reach_cells - out_row).astype(jnp.float32)
    weight = jnp.where(distance <= reach_cells, jnp.exp(-distance * rates[:, None] / reach_cells), 0.0)
    return weight.astype(jnp.bfloat16)


def along_x(padded, kernel):
    block_count = kernel.shape[1]
    reach_cells = kernel.shape[2]
    leading = padded.shape[:-1]
    blocks = padded.reshape(leading + (block_count + 2, reach_cells))
    summed = jnp.zeros(leading + (block_count, reach_cells), jnp.float32)
    for block_shift in range(3):
        summed = summed + jnp.einsum('abcnp,npq->abcnq', blocks[:, :, :, block_shift:block_shift + block_count, :], kernel[block_shift])
    return summed.reshape(leading + (block_count * reach_cells,))


def reference(control, forcing, obs_tile, obs_cell, obs_value, obs_count, rate_x, rate_y, vert):
    per_row = N_RX * OBS_DEV
    tile_ids = obs_tile[:, 0].reshape(N_RY, per_row)
    cell_ids = obs_cell.reshape(N_RY, per_row)
    values = jnp.moveaxis(obs_value.reshape(C, N_RY, per_row), 1, 0)
    counts = obs_count.reshape(N_RY, N_RX)
    forcing_rows = jnp.moveaxis(forcing.reshape(C, LEV, N_RY, CY, NX), 2, 0)
    slot_ids = jnp.arange(per_row) % OBS_DEV
    owner_ids = jnp.arange(per_row) // OBS_DEV
    kernel_x = band_kernel(rate_x, HX).astype(jnp.float32)

    def one_row(inputs):
        row_tiles, row_cells, row_values, row_counts, row_forcing = inputs
        usable = slot_ids < row_counts[owner_ids]
        level_ids = row_cells // (CY * CX)
        row_ids = (row_cells // CX) % CY
        col_ids = row_cells % CX
        flat_ids = level_ids * (CY * NX) + row_ids * NX + row_tiles * CX + col_ids
        kept_values = jnp.where(usable[None, :], row_values, 0.0)
        base = row_forcing.astype(jnp.float32).reshape(C, LEV * CY * NX)
        scatter_field = base.at[:, flat_ids].add(kept_values)
        observed = scatter_field.astype(jnp.bfloat16).reshape(C, LEV, CY, NX)
        padded = jnp.pad(observed, ((0, 0), (0, 0), (0, 0), (HX, HX))).astype(jnp.float32)
        return along_x(padded, kernel_x).astype(jnp.bfloat16)

    filtered = lax.map(one_row, (tile_ids, cell_ids, values, counts, forcing_rows))
    vert_wide = vert.astype(jnp.float32)
    zero_rim = jnp.zeros((C, LEV, HY, NX), filtered.dtype)

    def one_band(band_idx):
        lower_rim = jnp.where(band_idx > 0, filtered[jnp.maximum(band_idx - 1, 0)][:, :, CY - HY:, :], zero_rim)
        upper_rim = jnp.where(band_idx < N_RY - 1, filtered[jnp.minimum(band_idx + 1, N_RY - 1)][:, :, :HY, :], zero_rim)
        padded = jnp.concatenate([lower_rim, filtered[band_idx], upper_rim], axis=2).astype(jnp.float32)
        band_rates = lax.dynamic_slice_in_dim(rate_y, (band_idx * CY).astype(jnp.int32), CY)
        weights = lat_kernel(band_rates, HY).astype(jnp.float32)
        smooth = jnp.einsum('yp,clpx->clyx', weights, padded).astype(jnp.bfloat16)
        columns = jnp.einsum('clm,cmyx->clyx', vert_wide, smooth.astype(jnp.float32))
        control_band = lax.dynamic_slice_in_dim(control, (band_idx * CY).astype(jnp.int32), CY, 2).astype(jnp.float32)
        return (control_band + columns).astype(jnp.bfloat16)

    band_out = lax.map(one_band, jnp.arange(N_RY, dtype=jnp.int32))
    return jnp.moveaxis(band_out, 0, 2).reshape(C, LEV, NY, NX)
```

```python
import functools

import jax
import jax.numpy as jnp
from jax import lax
from jax.experimental import pallas as pl
from jax.experimental.pallas import tpu as pltpu
from jax.sharding import PartitionSpec as P

LEV = 64
CY = 8
CX = 128
SLOTS = 1024
ROWS = LEV * CY
TILES = 16
CHUNK = 256
VMEM = pl.BlockSpec(memory_space=pltpu.VMEM)
SMEM = pl.BlockSpec(memory_space=pltpu.SMEM)
F32 = jnp.float32
BF16 = jnp.bfloat16


def iota(shape, axis):
    return lax.broadcasted_iota(jnp.int32, shape, axis)


def pack_kernel(count_ref, tile_ref, cell_ref, value_ref, out_ref):
    used = iota((1, SLOTS), 1) < count_ref[0]
    cell = cell_ref[...]
    place = (cell // CX).astype(F32)
    column = (tile_ref[...] * CX + cell % CX).astype(F32)
    values = jnp.where(used, value_ref[...], 0.0)
    block = jnp.concatenate([place, column, values], axis=0)
    for tile in range(TILES):
        out_ref[tile] = block


def factors_kernel(where_ref, rate_y_ref, rate_x_ref, vert_ref, x_ref, rate_ref, y_ref):
    band, bands = where_ref[0], where_ref[1]
    tile, tiles = where_ref[2], where_ref[3]
    rates = rate_x_ref[...]
    source = iota((CX, CX), 0)
    target = iota((CX, CX), 1)
    for part in range(3):
        far = jnp.abs(source + (part - 1) * CX - target)
        near = far <= CX
        if part == 0:
            near = jnp.logical_and(near, tile > 0)
        if part == 2:
            near = jnp.logical_and(near, tile < tiles - 1)
        weight = jnp.where(near, jnp.exp(-far.astype(F32) * rates / CX), 0.0)
        x_ref[part * CX : (part + 1) * CX, :] = weight.astype(BF16)
    rate_ref[...] = jnp.broadcast_to(-rates / CX, (CX, CX)).T

    row = iota((CY, CX), 0)
    other = iota((CY, CX), 1) % CY
    rate = jnp.zeros((CY, CX), F32)
    for y in range(CY):
        rate = jnp.where(row == y, rate_y_ref[y], rate)
    spread = (iota((ROWS, LEV), 0) // CY == iota((ROWS, LEV), 1)).astype(BF16)
    weights = []
    for part in range(3):
        far = jnp.abs(other + (part - 1) * CY - row)
        near = far <= CY
        if part == 0:
            near = jnp.logical_and(near, band > 0)
        if part == 2:
            near = jnp.logical_and(near, band < bands - 1)
        weight = jnp.where(near, jnp.exp(-far.astype(F32) * rate / CY), 0.0)
        weights.append(weight.astype(BF16).astype(F32))
    for c in range(2):
        tall = jnp.dot(spread, vert_ref[c], preferred_element_type=F32).astype(BF16)
        wide = lax.dot_general(tall, spread, (((1,), (1,)), ((), ())), preferred_element_type=F32)
        wide = wide.reshape(LEV, CY, ROWS)
        for part in range(3):
            weight = jnp.concatenate([weights[part]] * (ROWS // CX), axis=1)
            product = (wide * weight[None]).reshape(ROWS, ROWS)
            y_ref[c, :, part * ROWS : (part + 1) * ROWS] = product.astype(BF16)


def lon_kernel(where_ref, record_ref, own_ref, left_ref, right_ref, x_ref, rate_ref, out_ref, sum_ref):
    start = (where_ref[2] * CX).astype(F32)
    places = iota((ROWS, CHUNK), 0).astype(F32)
    columns = iota((CX, CHUNK), 0).astype(F32) + start
    rate = rate_ref[:, 0:1]
    sum_ref[...] = jnp.zeros_like(sum_ref)

    def step(source, carry):
        for chunk in range(SLOTS // CHUNK):
            at = slice(chunk * CHUNK, (chunk + 1) * CHUNK)
            record = record_ref[source, :, at]
            hit = jnp.where(places == record[0:1], 1.0, 0.0).astype(BF16)
            far = jnp.abs(columns - record[1:2])
            weight = jnp.where(far <= CX, jnp.exp(far * rate), 0.0)
            spread = jnp.concatenate([weight * record[2:3], weight * record[3:4]], axis=0)
            sum_ref[...] += lax.dot_general(
                hit, spread.astype(BF16), (((1,), (1,)), ((), ())), preferred_element_type=F32
            )
        return carry

    lax.fori_loop(0, TILES, step, 0)
    for c in range(2):
        at = slice(c * ROWS, (c + 1) * ROWS)
        dense = jnp.dot(left_ref[at], x_ref[0:CX], preferred_element_type=F32)
        dense += jnp.dot(own_ref[at], x_ref[CX : 2 * CX], preferred_element_type=F32)
        dense += jnp.dot(right_ref[at], x_ref[2 * CX :], preferred_element_type=F32)
        out_ref[at] = (dense + sum_ref[:, c * CX : (c + 1) * CX]).astype(BF16)


def final_kernel(control_ref, lower_ref, own_ref, upper_ref, y_ref, out_ref):
    for c in range(2):
        at = slice(c * ROWS, (c + 1) * ROWS)
        total = control_ref[at].astype(F32)
        for part, field in enumerate((lower_ref, own_ref, upper_ref)):
            total += jnp.dot(
                y_ref[c, :, part * ROWS : (part + 1) * ROWS], field[at], preferred_element_type=F32
            )
        out_ref[at] = total.astype(BF16)


def ring(axis, step):
    count = lax.axis_size(axis)
    return [(i, (i + step) % count) for i in range(count)]


def call(kernel, out_shape, specs, scratch=(), flops=0, moved=0):
    many = isinstance(out_shape, (list, tuple))
    return pl.pallas_call(
        kernel,
        out_shape=out_shape,
        in_specs=specs,
        out_specs=[VMEM] * len(out_shape) if many else VMEM,
        scratch_shapes=list(scratch),
        cost_estimate=pl.CostEstimate(flops=flops, bytes_accessed=moved, transcendentals=0),
        compiler_params=pltpu.CompilerParams(vmem_limit_bytes=32 * 2**20),
    )


def body(control, forcing, obs_tile, obs_cell, obs_value, obs_count, rate_x, rate_y, vert):
    shape = control.shape
    band, tile = lax.axis_index("ry"), lax.axis_index("rx")
    where = jnp.stack([band, lax.axis_size("ry"), tile, lax.axis_size("rx")]).astype(jnp.int32)
    field = jax.ShapeDtypeStruct((2 * ROWS, CX), BF16)

    packed = call(
        pack_kernel, jax.ShapeDtypeStruct((TILES, 4, SLOTS), F32), [SMEM, VMEM, VMEM, VMEM], moved=300000
    )(obs_count, obs_tile.reshape(1, SLOTS), obs_cell.reshape(1, SLOTS), obs_value)
    records = lax.all_to_all(packed, "rx", 0, 0, tiled=True)
    left = lax.ppermute(forcing, "rx", ring("rx", 1))
    right = lax.ppermute(forcing, "rx", ring("rx", -1))

    rate_here = lax.dynamic_slice_in_dim(rate_x, tile * CX, CX).reshape(1, CX)
    x_weights, rate_down, y_weights = call(
        factors_kernel,
        [
            jax.ShapeDtypeStruct((3 * CX, CX), BF16),
            jax.ShapeDtypeStruct((CX, CX), F32),
            jax.ShapeDtypeStruct((2, ROWS, 3 * ROWS), BF16),
        ],
        [SMEM, SMEM, VMEM, VMEM],
        flops=2 * 512 * 512 * 64 * 2 * 2,
        moved=4000000,
    )(where, rate_y, rate_here, vert)

    flat = (2 * ROWS, CX)
    smooth = call(
        lon_kernel,
        field,
        [SMEM] + [VMEM] * 6,
        [pltpu.VMEM((ROWS, 2 * CX), F32)],
        flops=2 * ROWS * 256 * TILES * SLOTS,
        moved=1000000,
    )(where, records, forcing.reshape(flat), left.reshape(flat), right.reshape(flat), x_weights, rate_down)

    wide = smooth.reshape(shape)
    lower = lax.ppermute(wide, "ry", ring("ry", 1))
    upper = lax.ppermute(wide, "ry", ring("ry", -1))
    out = call(final_kernel, field, [VMEM] * 5, flops=2 * 2 * ROWS * 3 * ROWS * CX, moved=4000000)(
        control.reshape(flat), lower.reshape(flat), smooth, upper.reshape(flat), y_weights
    )
    return out.reshape(shape)


def solution(mesh):
    placed = (
        P(None, None, "ry", "rx"),
        P(None, None, "ry", "rx"),
        P(("ry", "rx"), None),
        P(("ry", "rx")),
        P(None, ("ry", "rx")),
        P(("ry", "rx")),
        P(),
        P("ry"),
        P(),
    )
    return jax.shard_map(
        body, mesh=mesh, in_specs=placed, out_specs=P(None, None, "ry", "rx"), check_vma=False
    )
```

```python
import jax
import jax.numpy as jnp
from jax import lax
from jax.experimental import pallas as pl
from jax.experimental.pallas import tpu as pltpu
from jax.sharding import PartitionSpec as P

LEV = 64
CY = 8
CX = 128
SLOTS = 1024
ROWS = LEV * CY
TILES = 16
PARTS = SLOTS // CX
VMEM = pl.BlockSpec(memory_space=pltpu.VMEM)
HBM = pl.BlockSpec(memory_space=pltpu.HBM)
F32 = jnp.float32
BF16 = jnp.bfloat16
I32 = jnp.int32
ACROSS = (((1,), (1,)), ((), ()))


def iota(shape, axis):
    return lax.broadcasted_iota(I32, shape, axis)


def pack_kernel(count_ref, place_ref, value_ref, out_ref, field_ref, lane_ref):
    before = (iota((CX, CX), 0) <= iota((CX, CX), 1)).astype(F32).astype(BF16)
    above = (iota((CX, CX), 0) > iota((CX, CX), 1)).astype(F32).astype(BF16)
    slot = iota((PARTS, CX), 0) * CX + iota((PARTS, CX), 1)
    used = slot < count_ref[...]
    tile = jnp.where(used, place_ref[0], -1)
    cell = place_ref[1]
    fields = [
        (cell // CX - ROWS // 2).astype(F32),
        (tile + 1).astype(F32),
        (cell % CX - CX // 2).astype(F32),
        value_ref[0:1].reshape(PARTS, CX),
        value_ref[1:2].reshape(PARTS, CX),
    ]

    named = jnp.concatenate([jnp.where(tile == t, 1.0, 0.0) for t in range(TILES)], axis=0)
    within = jnp.dot(named.astype(BF16), before, preferred_element_type=F32)
    counts = jnp.broadcast_to(within[:, CX - 1 :], (CX, CX)).astype(BF16)
    rank = named * (within + jnp.dot(above, counts, preferred_element_type=F32) - 1.0)
    rank = jnp.sum(rank.reshape(TILES, PARTS, CX), axis=0)
    rank = jnp.where(used, rank, float(SLOTS)).astype(I32)

    row, lane = rank // CX, rank % CX
    for part in range(PARTS):
        at = slice(part * CX, (part + 1) * CX)
        here = iota((PARTS, CX), 0) == row[part : part + 1]
        for i, field in enumerate(fields):
            picked = jnp.where(here, field[part : part + 1], 0.0)
            field_ref[i * PARTS : (i + 1) * PARTS, at] = picked.astype(BF16)
        lane_ref[:, at] = jnp.where(iota((CX, CX), 0) == lane[part : part + 1], 1.0, 0.0).astype(BF16)
    ordered = lax.dot_general(field_ref[...], lane_ref[...], ACROSS, preferred_element_type=F32)
    place, named, column, first, second = (ordered[i * PARTS : (i + 1) * PARTS] for i in range(5))
    column = jnp.where(named > 0.0, (named - 1.0) * CX + column, 4.0 * TILES * CX)
    for t in range(TILES):
        out_ref[t] = jnp.concatenate([place, column - t * CX, first, second], axis=0).astype(BF16)


def lon_kernel(
    record_ref, own_hbm, rate_x_hbm, sum_ref, x_ref, own_ref, rate_x_ref, rate_ref, list_ref, hit_ref, spread_ref, sems
):
    copies = [
        pltpu.make_async_copy(rate_x_hbm, rate_x_ref, sems.at[0]),
        pltpu.make_async_copy(own_hbm, own_ref, sems.at[1]),
    ]
    for copy in copies:
        copy.start()

    rows = TILES * PARTS
    field = lambda f: record_ref[:, f * PARTS : (f + 1) * PARTS, :].reshape(rows, CX)
    column = field(1).astype(F32)
    reached = jnp.logical_and(column >= -1.5 * CX, column < 1.5 * CX)
    some = jnp.max(jnp.where(reached, 1.0, 0.0), axis=1, keepdims=True)
    some = jnp.broadcast_to(some, (rows, CX)).astype(BF16)
    across = (((0,), (0,)), ((), ()))
    upto = (iota((rows, rows), 0) <= iota((rows, rows), 1)).astype(F32).astype(BF16)
    under = (iota((rows, rows), 0) < iota((rows, rows), 1)).astype(F32).astype(BF16)
    upto = lax.dot_general(some, upto, across, preferred_element_type=F32)
    under = lax.dot_general(some, under, across, preferred_element_type=F32)
    target_row = iota((rows, rows), 0).astype(F32)
    moved = jnp.logical_and(under == target_row, upto == target_row + 1.0)
    moved = jnp.where(moved, 1.0, 0.0).astype(BF16)
    for f in range(4):
        list_ref[f] = jnp.dot(moved, field(f), preferred_element_type=F32)
    used_rows = jnp.max(upto).astype(I32)

    tile, tiles = lax.axis_index("rx"), lax.axis_size("rx")
    copies[0].wait()
    rates = rate_x_ref[pl.ds(tile, 1), :]
    source = iota((CX, CX), 0)
    target = iota((CX, CX), 1)
    weights = []
    for part in range(3):
        far = jnp.abs(source + (part - 1) * CX - target)
        near = far <= CX
        if part == 0:
            near = jnp.logical_and(near, tile > 0)
        if part == 2:
            near = jnp.logical_and(near, tile < tiles - 1)
        weights.append(jnp.where(near, jnp.exp(-far.astype(F32) * rates / CX), 0.0))
    even = tile % 2 == 0
    x_ref[0:CX] = jnp.where(even, weights[2], weights[0]).astype(BF16)
    x_ref[CX : 2 * CX] = jnp.where(even, weights[0], weights[2]).astype(BF16)
    middle = weights[1].astype(BF16)
    rate_ref[...] = jnp.broadcast_to(rates * (-1.0 / CX), (CX, CX)).T
    copies[1].wait()
    for c in range(2):
        sum_ref[:, c * CX : (c + 1) * CX] = jnp.dot(
            own_ref[c * ROWS : (c + 1) * ROWS], middle, preferred_element_type=F32
        )

    def step(i, carry):
        record = list_ref[:, pl.ds(pl.multiple_of(i * PARTS, PARTS), PARTS), :]
        places = iota((ROWS, CX), 0) - ROWS // 2
        columns = (iota((CX, CX), 0) - CX // 2).astype(F32)
        for part in range(PARTS):
            at = slice(part * CX, (part + 1) * CX)
            row = lambda f: record[f, part : part + 1]
            hit_ref[:, at] = jnp.where(places == row(0).astype(I32), 1.0, 0.0).astype(BF16)
            far = jnp.abs(columns - row(1))
            weight = jnp.where(far <= CX, jnp.exp(far * rate_ref[...]), 0.0)
            for c in range(2):
                spread_ref[c * CX : (c + 1) * CX, at] = (weight * row(2 + c)).astype(BF16)
        sum_ref[...] += lax.dot_general(hit_ref[...], spread_ref[...], ACROSS, preferred_element_type=F32)
        return carry

    lax.fori_loop(0, (used_rows + PARTS - 1) // PARTS, step, 0)


def dense_kernel(sum_ref, near_ref, far_ref, x_ref, out_ref):
    for c in range(2):
        at = slice(c * ROWS, (c + 1) * ROWS)
        total = sum_ref[:, c * CX : (c + 1) * CX]
        total += jnp.dot(near_ref[at], x_ref[0:CX], preferred_element_type=F32)
        total += jnp.dot(far_ref[at], x_ref[CX : 2 * CX], preferred_element_type=F32)
        out_ref[at] = total.astype(BF16)


def own_kernel(smooth_ref, control_ref, rate_y_ref, vert_ref, total_ref, y_ref):
    band, bands = lax.axis_index("ry"), lax.axis_size("ry")
    row = iota((CY, CX), 0)
    other = iota((CY, CX), 1) % CY
    rate = jnp.zeros((CY, CX), F32)
    for y in range(CY):
        rate = jnp.where(row == y, rate_y_ref[0:1, y : y + 1], rate)
    spread = (iota((ROWS, LEV), 0) // CY == iota((ROWS, LEV), 1)).astype(BF16)
    weights = []
    for part in range(3):
        far = jnp.abs(other + (part - 1) * CY - row)
        near = far <= CY
        if part == 0:
            near = jnp.logical_and(near, band > 0)
        if part == 2:
            near = jnp.logical_and(near, band < bands - 1)
        weight = jnp.where(near, jnp.exp(-far.astype(F32) * rate / CY), 0.0)
        weights.append(jnp.concatenate([weight.astype(BF16).astype(F32)] * (ROWS // CX), axis=1))
    for c in range(2):
        at = slice(c * ROWS, (c + 1) * ROWS)
        tall = jnp.dot(spread, vert_ref[c], preferred_element_type=F32).astype(BF16)
        wide = lax.dot_general(tall, spread, ACROSS, preferred_element_type=F32).reshape(LEV, CY, ROWS)
        for part in (0, 2):
            product = (wide * weights[part][None]).reshape(ROWS, ROWS)
            y_ref[c, :, part // 2 * ROWS : (part // 2 + 1) * ROWS] = product.astype(BF16)
        middle = (wide * weights[1][None]).reshape(ROWS, ROWS).astype(BF16)
        mixed = jnp.dot(middle, smooth_ref[at], preferred_element_type=F32)
        total_ref[at] = control_ref[at].astype(F32) + mixed


def final_kernel(total_ref, lower_ref, upper_ref, y_ref, out_ref):
    for c in range(2):
        at = slice(c * ROWS, (c + 1) * ROWS)
        total = total_ref[at]
        total += jnp.dot(y_ref[c, :, 0:ROWS], lower_ref[at], preferred_element_type=F32)
        total += jnp.dot(y_ref[c, :, ROWS:], upper_ref[at], preferred_element_type=F32)
        out_ref[at] = total.astype(BF16)


def call(kernel, out_shape, specs, scratch=(), flops=0, moved=0, limit=24):
    many = isinstance(out_shape, (list, tuple))
    return pl.pallas_call(
        kernel,
        out_shape=out_shape,
        in_specs=specs,
        out_specs=[VMEM] * len(out_shape) if many else VMEM,
        scratch_shapes=list(scratch),
        cost_estimate=pl.CostEstimate(flops=flops, bytes_accessed=moved, transcendentals=0),
        compiler_params=pltpu.CompilerParams(vmem_limit_bytes=limit * 2**20),
    )


def body(control, forcing, obs_tile, obs_cell, obs_value, obs_count, rate_x, rate_y, vert):
    shape = control.shape
    flat = (2 * ROWS, CX)
    bands, tiles = lax.axis_size("ry"), lax.axis_size("rx")
    struct = jax.ShapeDtypeStruct

    places = jnp.stack([obs_tile.reshape(PARTS, CX), obs_cell.reshape(PARTS, CX)])
    packed = call(
        pack_kernel,
        struct((TILES, 4 * PARTS, CX), BF16),
        [VMEM] * 3,
        [pltpu.VMEM((5 * PARTS, SLOTS), BF16), pltpu.VMEM((CX, SLOTS), BF16)],
        flops=3 * 10**9,
        moved=200000,
    )(obs_count.reshape(1, 1), places, obs_value)
    records = lax.all_to_all(packed, "rx", 0, 0, tiled=True)

    held, _ = lax.optimization_barrier((forcing, packed))
    inner = lax.ppermute(held, "rx", [(i, i ^ 1) for i in range(tiles)])
    outer = lax.ppermute(held, "rx", [(i, ((i + 1) ^ 1) - 1) for i in range(1, tiles - 1)])

    total, x_weights = call(
        lon_kernel,
        [struct((ROWS, 2 * CX), F32), struct((2 * CX, CX), BF16)],
        [VMEM, HBM, HBM],
        [
            pltpu.VMEM(flat, BF16),
            pltpu.VMEM((TILES, CX), F32),
            pltpu.VMEM((CX, CX), F32),
            pltpu.VMEM((4, TILES * PARTS, CX), F32),
            pltpu.VMEM((ROWS, SLOTS), BF16),
            pltpu.VMEM((2 * CX, SLOTS), BF16),
            pltpu.SemaphoreType.DMA((2,)),
        ],
        flops=2 * ROWS * 256 * TILES * SLOTS,
        moved=1000000,
    )(records, forcing.reshape(flat), rate_x.reshape(TILES, CX))

    smooth = call(dense_kernel, struct(flat, BF16), [VMEM] * 4, flops=2 * 1024 * 256 * 128, moved=1000000)(
        total, inner.reshape(flat), outer.reshape(flat), x_weights
    )
    wide = smooth.reshape(shape)
    lower = lax.ppermute(wide, "ry", [(i, i + 1) for i in range(bands - 1)])
    upper = lax.ppermute(wide, "ry", [(i + 1, i) for i in range(bands - 1)])
    total, y_weights = call(
        own_kernel,
        [struct(flat, F32), struct((2, ROWS, 2 * ROWS), BF16)],
        [VMEM] * 4,
        flops=2 * 2 * ROWS * ROWS * CX * 2,
        moved=4000000,
    )(smooth, control.reshape(flat), rate_y.reshape(1, CY), vert)
    out = call(final_kernel, struct(flat, BF16), [VMEM] * 4, flops=2 * 2 * ROWS * 2 * ROWS * CX, moved=4000000)(
        total, lower.reshape(flat), upper.reshape(flat), y_weights
    )
    return out.reshape(shape)


def solution(mesh):
    placed = (
        P(None, None, "ry", "rx"),
        P(None, None, "ry", "rx"),
        P(("ry", "rx"), None),
        P(("ry", "rx")),
        P(None, ("ry", "rx")),
        P(("ry", "rx")),
        P(),
        P("ry"),
        P(),
    )
    return jax.shard_map(
        body, mesh=mesh, in_specs=placed, out_specs=P(None, None, "ry", "rx"), check_vma=False
    )
```

```python
import functools

import jax
import jax.numpy as jnp
from jax import lax
from jax.experimental import pallas as pl
from jax.experimental.pallas import tpu as pltpu
from jax.sharding import PartitionSpec as P

LEV = 64
CY = 8
CX = 128
SLOTS = 1024
ROWS = LEV * CY
TILES = 16
PARTS = SLOTS // CX
VMEM = pl.BlockSpec(memory_space=pltpu.VMEM)
HBM = pl.BlockSpec(memory_space=pltpu.HBM)
F32 = jnp.float32
BF16 = jnp.bfloat16
I32 = jnp.int32
ACROSS = (((1,), (1,)), ((), ()))


def iota(shape, axis):
    return lax.broadcasted_iota(I32, shape, axis)


def pack_kernel(count_ref, place_ref, value_ref, out_ref, field_ref, lane_ref):
    before = (iota((CX, CX), 0) <= iota((CX, CX), 1)).astype(F32).astype(BF16)
    above = (iota((CX, CX), 0) > iota((CX, CX), 1)).astype(F32).astype(BF16)
    slot = iota((PARTS, CX), 0) * CX + iota((PARTS, CX), 1)
    used = slot < count_ref[...]
    tile = jnp.where(used, place_ref[0], -1)
    cell = place_ref[1]
    fields = [
        (cell // CX - ROWS // 2).astype(F32),
        (tile + 1).astype(F32),
        (cell % CX - CX // 2).astype(F32),
        value_ref[0:1].reshape(PARTS, CX),
        value_ref[1:2].reshape(PARTS, CX),
    ]

    named = jnp.concatenate([jnp.where(tile == t, 1.0, 0.0) for t in range(TILES)], axis=0)
    within = jnp.dot(named.astype(BF16), before, preferred_element_type=F32)
    counts = jnp.broadcast_to(within[:, CX - 1 :], (CX, CX)).astype(BF16)
    rank = named * (within + jnp.dot(above, counts, preferred_element_type=F32) - 1.0)
    rank = jnp.sum(rank.reshape(TILES, PARTS, CX), axis=0)
    rank = jnp.where(used, rank, float(SLOTS)).astype(I32)

    row, lane = rank // CX, rank % CX
    for part in range(PARTS):
        at = slice(part * CX, (part + 1) * CX)
        here = iota((PARTS, CX), 0) == row[part : part + 1]
        for i, field in enumerate(fields):
            picked = jnp.where(here, field[part : part + 1], 0.0)
            field_ref[i * PARTS : (i + 1) * PARTS, at] = picked.astype(BF16)
        lane_ref[:, at] = jnp.where(iota((CX, CX), 0) == lane[part : part + 1], 1.0, 0.0).astype(BF16)
    ordered = lax.dot_general(field_ref[...], lane_ref[...], ACROSS, preferred_element_type=F32)
    place, named, column, first, second = (ordered[i * PARTS : (i + 1) * PARTS] for i in range(5))
    column = jnp.where(named > 0.0, (named - 1.0) * CX + column, 4.0 * TILES * CX)
    for t in range(TILES):
        out_ref[t] = jnp.concatenate([place, column - t * CX, first, second], axis=0).astype(BF16)


def lon_kernel(
    record_ref, own_hbm, rate_x_hbm, sum_ref, x_ref, own_ref, rate_x_ref, rate_ref, list_ref, sems
):
    copies = [
        pltpu.make_async_copy(rate_x_hbm, rate_x_ref, sems.at[0]),
        pltpu.make_async_copy(own_hbm, own_ref, sems.at[1]),
    ]
    for copy in copies:
        copy.start()

    rows = TILES * PARTS
    field = lambda f: record_ref[:, f * PARTS : (f + 1) * PARTS, :].reshape(rows, CX)
    column = field(1).astype(F32)
    reached = jnp.logical_and(column >= -1.5 * CX, column < 1.5 * CX)
    some = jnp.max(jnp.where(reached, 1.0, 0.0), axis=1, keepdims=True)
    some = jnp.broadcast_to(some, (rows, CX)).astype(BF16)
    across = (((0,), (0,)), ((), ()))
    upto = (iota((rows, rows), 0) <= iota((rows, rows), 1)).astype(F32).astype(BF16)
    under = (iota((rows, rows), 0) < iota((rows, rows), 1)).astype(F32).astype(BF16)
    upto = lax.dot_general(some, upto, across, preferred_element_type=F32)
    under = lax.dot_general(some, under, across, preferred_element_type=F32)
    target_row = iota((rows, rows), 0).astype(F32)
    moved = jnp.logical_and(under == target_row, upto == target_row + 1.0)
    moved = jnp.where(moved, 1.0, 0.0).astype(BF16)
    for f in range(4):
        list_ref[f] = jnp.dot(moved, field(f), preferred_element_type=F32)
    used_rows = jnp.max(upto).astype(I32)

    tile, tiles = lax.axis_index("rx"), lax.axis_size("rx")
    copies[0].wait()
    rates = rate_x_ref[pl.ds(tile, 1), :]
    source = iota((CX, CX), 0)
    target = iota((CX, CX), 1)
    weights = []
    for part in range(3):
        far = jnp.abs(source + (part - 1) * CX - target)
        near = far <= CX
        if part == 0:
            near = jnp.logical_and(near, tile > 0)
        if part == 2:
            near = jnp.logical_and(near, tile < tiles - 1)
        weights.append(jnp.where(near, jnp.exp(-far.astype(F32) * rates / CX), 0.0))
    even = tile % 2 == 0
    x_ref[0:CX] = jnp.where(even, weights[2], weights[0]).astype(BF16)
    x_ref[CX : 2 * CX] = jnp.where(even, weights[0], weights[2]).astype(BF16)
    middle = weights[1].astype(BF16)
    rate_ref[...] = jnp.broadcast_to(rates * (-1.0 / CX), (CX, CX)).T
    copies[1].wait()
    for c in range(2):
        sum_ref[:, c * CX : (c + 1) * CX] = jnp.dot(
            own_ref[c * ROWS : (c + 1) * ROWS], middle, preferred_element_type=F32
        )

    def add(start):
        record = list_ref[:, pl.ds(pl.multiple_of(start, PARTS), PARTS), :]
        places = iota((ROWS, CX), 0) - ROWS // 2
        columns = (iota((CX, CX), 0) - CX // 2).astype(F32)
        hits, spreads = [], []
        for part in range(PARTS):
            place, column, first, second = (record[f, part : part + 1] for f in range(4))
            hits.append(jnp.where(places == place.astype(I32), 1.0, 0.0).astype(BF16))
            far = jnp.abs(columns - column)
            weight = jnp.where(far <= CX, jnp.exp(far * rate_ref[...]), 0.0)
            spreads.append(jnp.concatenate([weight * first, weight * second], axis=0).astype(BF16))
        sum_ref[...] += lax.dot_general(
            jnp.concatenate(hits, axis=1), jnp.concatenate(spreads, axis=1), ACROSS, preferred_element_type=F32
        )

    def step(i, carry):
        add(2 * PARTS * i)
        add(2 * PARTS * i + PARTS)
        return carry

    lax.fori_loop(0, (used_rows + 2 * PARTS - 1) // (2 * PARTS), step, 0)


def dense_kernel(sum_ref, near_ref, far_ref, x_ref, out_ref):
    for c in range(2):
        at = slice(c * ROWS, (c + 1) * ROWS)
        total = sum_ref[:, c * CX : (c + 1) * CX]
        total += jnp.dot(near_ref[at], x_ref[0:CX], preferred_element_type=F32)
        total += jnp.dot(far_ref[at], x_ref[CX : 2 * CX], preferred_element_type=F32)
        out_ref[at] = total.astype(BF16)


def own_kernel(smooth_ref, control_ref, rate_y_ref, vert_ref, total_ref, y_ref):
    band, bands = lax.axis_index("ry"), lax.axis_size("ry")
    row = iota((CY, CX), 0)
    other = iota((CY, CX), 1) % CY
    rate = jnp.zeros((CY, CX), F32)
    for y in range(CY):
        rate = jnp.where(row == y, rate_y_ref[0:1, y : y + 1], rate)
    spread = (iota((ROWS, LEV), 0) // CY == iota((ROWS, LEV), 1)).astype(BF16)
    weights = []
    for part in range(3):
        far = jnp.abs(other + (part - 1) * CY - row)
        near = far <= CY
        if part == 0:
            near = jnp.logical_and(near, band > 0)
        if part == 2:
            near = jnp.logical_and(near, band < bands - 1)
        weight = jnp.where(near, jnp.exp(-far.astype(F32) * rate / CY), 0.0)
        weights.append(jnp.concatenate([weight.astype(BF16).astype(F32)] * (ROWS // CX), axis=1))
    even = band % 2 == 0
    weights = [jnp.where(even, weights[2], weights[0]), weights[1], jnp.where(even, weights[0], weights[2])]
    for c in range(2):
        at = slice(c * ROWS, (c + 1) * ROWS)
        tall = jnp.dot(spread, vert_ref[c], preferred_element_type=F32).astype(BF16)
        wide = lax.dot_general(tall, spread, ACROSS, preferred_element_type=F32).reshape(LEV, CY, ROWS)
        for part in (0, 2):
            product = (wide * weights[part][None]).reshape(ROWS, ROWS)
            y_ref[part // 2, c] = product.astype(BF16)
        middle = (wide * weights[1][None]).reshape(ROWS, ROWS).astype(BF16)
        mixed = jnp.dot(middle, smooth_ref[at], preferred_element_type=F32)
        total_ref[at] = control_ref[at].astype(F32) + mixed


def band_kernel(part, total_ref, band_ref, y_ref, out_ref):
    for c in range(2):
        at = slice(c * ROWS, (c + 1) * ROWS)
        mixed = jnp.dot(y_ref[part, c], band_ref[at], preferred_element_type=F32)
        out_ref[at] = (total_ref[at] + mixed).astype(out_ref.dtype)


def call(kernel, out_shape, specs, scratch=(), flops=0, moved=0, limit=24):
    many = isinstance(out_shape, (list, tuple))
    return pl.pallas_call(
        kernel,
        out_shape=out_shape,
        in_specs=specs,
        out_specs=[VMEM] * len(out_shape) if many else VMEM,
        scratch_shapes=list(scratch),
        cost_estimate=pl.CostEstimate(flops=flops, bytes_accessed=moved, transcendentals=0),
        compiler_params=pltpu.CompilerParams(vmem_limit_bytes=limit * 2**20),
    )


def body(control, forcing, obs_tile, obs_cell, obs_value, obs_count, rate_x, rate_y, vert):
    shape = control.shape
    flat = (2 * ROWS, CX)
    bands, tiles = lax.axis_size("ry"), lax.axis_size("rx")
    struct = jax.ShapeDtypeStruct

    places = jnp.stack([obs_tile.reshape(PARTS, CX), obs_cell.reshape(PARTS, CX)])
    packed = call(
        pack_kernel,
        struct((TILES, 4 * PARTS, CX), BF16),
        [VMEM] * 3,
        [pltpu.VMEM((5 * PARTS, SLOTS), BF16), pltpu.VMEM((CX, SLOTS), BF16)],
        flops=3 * 10**9,
        moved=200000,
    )(obs_count.reshape(1, 1), places, obs_value)
    records = lax.all_to_all(packed, "rx", 0, 0, tiled=True)

    held, _ = lax.optimization_barrier((forcing, packed))
    inner = lax.ppermute(held, "rx", [(i, i ^ 1) for i in range(tiles)])
    outer = lax.ppermute(held, "rx", [(i, ((i + 1) ^ 1) - 1) for i in range(1, tiles - 1)])

    total, x_weights = call(
        lon_kernel,
        [struct((ROWS, 2 * CX), F32), struct((2 * CX, CX), BF16)],
        [VMEM, HBM, HBM],
        [
            pltpu.VMEM(flat, BF16),
            pltpu.VMEM((TILES, CX), F32),
            pltpu.VMEM((CX, CX), F32),
            pltpu.VMEM((4, TILES * PARTS, CX), F32),
            pltpu.SemaphoreType.DMA((2,)),
        ],
        flops=2 * ROWS * 256 * TILES * SLOTS,
        moved=1000000,
    )(records, forcing.reshape(flat), rate_x.reshape(TILES, CX))

    smooth = call(dense_kernel, struct(flat, BF16), [VMEM] * 4, flops=2 * 1024 * 256 * 128, moved=1000000)(
        total, inner.reshape(flat), outer.reshape(flat), x_weights
    )
    wide = smooth.reshape(shape)
    inner = lax.ppermute(wide, "ry", [(i, i ^ 1) for i in range(bands)])
    outer = lax.ppermute(wide, "ry", [(i, ((i + 1) ^ 1) - 1) for i in range(1, bands - 1)])
    total, y_weights = call(
        own_kernel,
        [struct(flat, F32), struct((2, 2, ROWS, ROWS), BF16)],
        [VMEM] * 4,
        flops=2 * 2 * ROWS * ROWS * CX * 2,
        moved=4000000,
    )(smooth, control.reshape(flat), rate_y.reshape(1, CY), vert)
    for part, band, dtype in ((0, inner, F32), (1, outer, BF16)):
        total = call(
            functools.partial(band_kernel, part),
            struct(flat, dtype),
            [VMEM] * 3,
            flops=2 * 2 * ROWS * ROWS * CX,
            moved=2000000,
        )(total, band.reshape(flat), y_weights)
    return total.reshape(shape)


def solution(mesh):
    placed = (
        P(None, None, "ry", "rx"),
        P(None, None, "ry", "rx"),
        P(("ry", "rx"), None),
        P(("ry", "rx")),
        P(None, ("ry", "rx")),
        P(("ry", "rx")),
        P(),
        P("ry"),
        P(),
    )
    return jax.shard_map(
        body, mesh=mesh, in_specs=placed, out_specs=P(None, None, "ry", "rx"), check_vma=False
    )
```

```python
import functools

import jax
import jax.numpy as jnp
from jax import lax
from jax.experimental import pallas as pl
from jax.experimental.pallas import tpu as pltpu
from jax.sharding import PartitionSpec as P

LEV = 64
CY = 8
CX = 128
SLOTS = 1024
ROWS = LEV * CY
TILES = 16
PARTS = SLOTS // CX
VMEM = pl.BlockSpec(memory_space=pltpu.VMEM)
HBM = pl.BlockSpec(memory_space=pltpu.HBM)
F32 = jnp.float32
BF16 = jnp.bfloat16
I32 = jnp.int32
ACROSS = (((1,), (1,)), ((), ()))


def iota(shape, axis):
    return lax.broadcasted_iota(I32, shape, axis)


def pack_kernel(
    count_ref, tile_hbm, cell_hbm, value_hbm, out_ref, tiles, cells, values, field_ref, lane_ref, sems
):
    pairs = ((tile_hbm, tiles), (cell_hbm, cells), (value_hbm, values))
    copies = [pltpu.make_async_copy(a, b, sems.at[i]) for i, (a, b) in enumerate(pairs)]
    for copy in copies:
        copy.start()
    before = (iota((CX, CX), 0) <= iota((CX, CX), 1)).astype(F32).astype(BF16)
    above = (iota((CX, CX), 0) > iota((CX, CX), 1)).astype(F32).astype(BF16)
    slot = iota((PARTS, CX), 0) * CX + iota((PARTS, CX), 1)
    for copy in copies:
        copy.wait()
    used = slot < count_ref[0]
    tile = jnp.where(used, tiles[...], -1)
    cell = cells[...]
    fields = [
        (cell // CX - ROWS // 2).astype(F32),
        (tile + 1).astype(F32),
        (cell % CX - CX // 2).astype(F32),
        values[0:1].reshape(PARTS, CX),
        values[1:2].reshape(PARTS, CX),
    ]

    named = jnp.concatenate([jnp.where(tile == t, 1.0, 0.0) for t in range(TILES)], axis=0)
    within = jnp.dot(named.astype(BF16), before, preferred_element_type=F32)
    counts = jnp.broadcast_to(within[:, CX - 1 :], (CX, CX)).astype(BF16)
    rank = named * (within + jnp.dot(above, counts, preferred_element_type=F32) - 1.0)
    rank = jnp.sum(rank.reshape(TILES, PARTS, CX), axis=0)
    rank = jnp.where(used, rank, float(SLOTS)).astype(I32)

    row, lane = rank // CX, rank % CX
    for part in range(PARTS):
        at = slice(part * CX, (part + 1) * CX)
        here = iota((PARTS, CX), 0) == row[part : part + 1]
        for i, field in enumerate(fields):
            picked = jnp.where(here, field[part : part + 1], 0.0)
            field_ref[i * PARTS : (i + 1) * PARTS, at] = picked.astype(BF16)
        lane_ref[:, at] = jnp.where(iota((CX, CX), 0) == lane[part : part + 1], 1.0, 0.0).astype(BF16)
    ordered = lax.dot_general(field_ref[...], lane_ref[...], ACROSS, preferred_element_type=F32)
    place, named, column, first, second = (ordered[i * PARTS : (i + 1) * PARTS] for i in range(5))
    column = jnp.where(named > 0.0, (named - 1.0) * CX + column, 4.0 * TILES * CX)
    for t in range(TILES):
        out_ref[t] = jnp.concatenate([place, column - t * CX, first, second], axis=0).astype(BF16)


def lon_kernel(
    record_ref, own_hbm, rate_x_hbm, sum_ref, x_ref, own_ref, rate_x_ref, rate_ref, list_ref, sems
):
    copies = [
        pltpu.make_async_copy(rate_x_hbm, rate_x_ref, sems.at[0]),
        pltpu.make_async_copy(own_hbm, own_ref, sems.at[1]),
    ]
    for copy in copies:
        copy.start()

    rows = TILES * PARTS
    field = lambda f: record_ref[:, f * PARTS : (f + 1) * PARTS, :].reshape(rows, CX)
    column = field(1).astype(F32)
    reached = jnp.logical_and(column >= -1.5 * CX, column < 1.5 * CX)
    some = jnp.max(jnp.where(reached, 1.0, 0.0), axis=1, keepdims=True)
    some = jnp.broadcast_to(some, (rows, CX)).astype(BF16)
    across = (((0,), (0,)), ((), ()))
    upto = (iota((rows, rows), 0) <= iota((rows, rows), 1)).astype(F32).astype(BF16)
    under = (iota((rows, rows), 0) < iota((rows, rows), 1)).astype(F32).astype(BF16)
    upto = lax.dot_general(some, upto, across, preferred_element_type=F32)
    under = lax.dot_general(some, under, across, preferred_element_type=F32)
    target_row = iota((rows, rows), 0).astype(F32)
    moved = jnp.logical_and(under == target_row, upto == target_row + 1.0)
    moved = jnp.where(moved, 1.0, 0.0).astype(BF16)
    for f in range(4):
        list_ref[f] = jnp.dot(moved, field(f), preferred_element_type=F32)
    used_rows = jnp.max(upto).astype(I32)

    tile, tiles = lax.axis_index("rx"), lax.axis_size("rx")
    copies[0].wait()
    rates = rate_x_ref[pl.ds(tile, 1), :]
    source = iota((CX, CX), 0)
    target = iota((CX, CX), 1)
    weights = []
    for part in range(3):
        far = jnp.abs(source + (part - 1) * CX - target)
        near = far <= CX
        if part == 0:
            near = jnp.logical_and(near, tile > 0)
        if part == 2:
            near = jnp.logical_and(near, tile < tiles - 1)
        weights.append(jnp.where(near, jnp.exp(-far.astype(F32) * rates / CX), 0.0))
    even = tile % 2 == 0
    x_ref[0:CX] = jnp.where(even, weights[2], weights[0]).astype(BF16)
    x_ref[CX : 2 * CX] = jnp.where(even, weights[0], weights[2]).astype(BF16)
    middle = weights[1].astype(BF16)
    rate_ref[...] = jnp.broadcast_to(rates * (-1.0 / CX), (CX, CX)).T
    copies[1].wait()
    for c in range(2):
        sum_ref[:, c * CX : (c + 1) * CX] = jnp.dot(
            own_ref[c * ROWS : (c + 1) * ROWS], middle, preferred_element_type=F32
        )

    def add(start):
        record = list_ref[:, pl.ds(pl.multiple_of(start, PARTS), PARTS), :]
        places = iota((ROWS, CX), 0) - ROWS // 2
        columns = (iota((CX, CX), 0) - CX // 2).astype(F32)
        hits, spreads = [], []
        for part in range(PARTS):
            place, column, first, second = (record[f, part : part + 1] for f in range(4))
            hits.append(jnp.where(places == place.astype(I32), 1.0, 0.0).astype(BF16))
            far = jnp.abs(columns - column)
            weight = jnp.where(far <= CX, jnp.exp(far * rate_ref[...]), 0.0)
            spreads.append(jnp.concatenate([weight * first, weight * second], axis=0).astype(BF16))
        sum_ref[...] += lax.dot_general(
            jnp.concatenate(hits, axis=1), jnp.concatenate(spreads, axis=1), ACROSS, preferred_element_type=F32
        )

    def step(i, carry):
        add(2 * PARTS * i)
        add(2 * PARTS * i + PARTS)
        return carry

    lax.fori_loop(0, (used_rows + 2 * PARTS - 1) // (2 * PARTS), step, 0)


def dense_kernel(sum_ref, near_ref, far_ref, x_ref, out_ref):
    for c in range(2):
        at = slice(c * ROWS, (c + 1) * ROWS)
        total = sum_ref[:, c * CX : (c + 1) * CX]
        total += jnp.dot(near_ref[at], x_ref[0:CX], preferred_element_type=F32)
        total += jnp.dot(far_ref[at], x_ref[CX : 2 * CX], preferred_element_type=F32)
        out_ref[at] = total.astype(BF16)


def own_kernel(smooth_ref, control_ref, rate_y_ref, vert_ref, total_ref, y_ref):
    band, bands = lax.axis_index("ry"), lax.axis_size("ry")
    row = iota((CY, CX), 0)
    other = iota((CY, CX), 1) % CY
    rate = jnp.zeros((CY, CX), F32)
    for y in range(CY):
        rate = jnp.where(row == y, rate_y_ref[0:1, y : y + 1], rate)
    spread = (iota((ROWS, LEV), 0) // CY == iota((ROWS, LEV), 1)).astype(BF16)
    weights = []
    for part in range(3):
        far = jnp.abs(other + (part - 1) * CY - row)
        near = far <= CY
        if part == 0:
            near = jnp.logical_and(near, band > 0)
        if part == 2:
            near = jnp.logical_and(near, band < bands - 1)
        weight = jnp.where(near, jnp.exp(-far.astype(F32) * rate / CY), 0.0)
        weights.append(jnp.concatenate([weight.astype(BF16).astype(F32)] * (ROWS // CX), axis=1))
    even = band % 2 == 0
    weights = [jnp.where(even, weights[2], weights[0]), weights[1], jnp.where(even, weights[0], weights[2])]
    for c in range(2):
        at = slice(c * ROWS, (c + 1) * ROWS)
        tall = jnp.dot(spread, vert_ref[c], preferred_element_type=F32).astype(BF16)
        wide = lax.dot_general(tall, spread, ACROSS, preferred_element_type=F32).reshape(LEV, CY, ROWS)
        for part in (0, 2):
            product = (wide * weights[part][None]).reshape(ROWS, ROWS)
            y_ref[part // 2, c] = product.astype(BF16)
        middle = (wide * weights[1][None]).reshape(ROWS, ROWS).astype(BF16)
        mixed = jnp.dot(middle, smooth_ref[at], preferred_element_type=F32)
        total_ref[at] = control_ref[at].astype(F32) + mixed


def band_kernel(part, total_ref, band_ref, y_ref, out_ref):
    for c in range(2):
        at = slice(c * ROWS, (c + 1) * ROWS)
        mixed = jnp.dot(y_ref[part, c], band_ref[at], preferred_element_type=F32)
        out_ref[at] = (total_ref[at] + mixed).astype(out_ref.dtype)


def call(kernel, out_shape, specs, scratch=(), flops=0, moved=0, limit=24):
    many = isinstance(out_shape, (list, tuple))
    return pl.pallas_call(
        kernel,
        out_shape=out_shape,
        in_specs=specs,
        out_specs=[VMEM] * len(out_shape) if many else VMEM,
        scratch_shapes=list(scratch),
        cost_estimate=pl.CostEstimate(flops=flops, bytes_accessed=moved, transcendentals=0),
        compiler_params=pltpu.CompilerParams(vmem_limit_bytes=limit * 2**20),
    )


def body(control, forcing, obs_tile, obs_cell, obs_value, obs_count, rate_x, rate_y, vert):
    shape = control.shape
    flat = (2 * ROWS, CX)
    bands, tiles = lax.axis_size("ry"), lax.axis_size("rx")
    struct = jax.ShapeDtypeStruct

    inputs = (obs_count, obs_tile.reshape(PARTS, CX), obs_cell.reshape(PARTS, CX), obs_value)
    packed = call(
        pack_kernel,
        struct((TILES, 4 * PARTS, CX), BF16),
        [pl.BlockSpec(memory_space=pltpu.SMEM)] + [HBM] * 3,
        [
            pltpu.VMEM((PARTS, CX), I32),
            pltpu.VMEM((PARTS, CX), I32),
            pltpu.VMEM((2, SLOTS), F32),
            pltpu.VMEM((5 * PARTS, SLOTS), BF16),
            pltpu.VMEM((CX, SLOTS), BF16),
            pltpu.SemaphoreType.DMA((3,)),
        ],
        flops=3 * 10**9,
        moved=200000,
    )(inputs[0], *(pltpu.with_memory_space_constraint(x, pltpu.HBM) for x in inputs[1:]))
    records = lax.all_to_all(packed, "rx", 0, 0, tiled=True)

    held, _ = lax.optimization_barrier((forcing, packed))
    inner = lax.ppermute(held, "rx", [(i, i ^ 1) for i in range(tiles)])
    outer = lax.ppermute(held, "rx", [(i, ((i + 1) ^ 1) - 1) for i in range(1, tiles - 1)])

    total, x_weights = call(
        lon_kernel,
        [struct((ROWS, 2 * CX), F32), struct((2 * CX, CX), BF16)],
        [VMEM, HBM, HBM],
        [
            pltpu.VMEM(flat, BF16),
            pltpu.VMEM((TILES, CX), F32),
            pltpu.VMEM((CX, CX), F32),
            pltpu.VMEM((4, TILES * PARTS, CX), F32),
            pltpu.SemaphoreType.DMA((2,)),
        ],
        flops=2 * ROWS * 256 * TILES * SLOTS,
        moved=1000000,
    )(records, forcing.reshape(flat), rate_x.reshape(TILES, CX))

    smooth = call(dense_kernel, struct(flat, BF16), [VMEM] * 4, flops=2 * 1024 * 256 * 128, moved=1000000)(
        total, inner.reshape(flat), outer.reshape(flat), x_weights
    )
    wide = smooth.reshape(shape)
    inner = lax.ppermute(wide, "ry", [(i, i ^ 1) for i in range(bands)])
    outer = lax.ppermute(wide, "ry", [(i, ((i + 1) ^ 1) - 1) for i in range(1, bands - 1)])
    total, y_weights = call(
        own_kernel,
        [struct(flat, F32), struct((2, 2, ROWS, ROWS), BF16)],
        [VMEM] * 4,
        flops=2 * 2 * ROWS * ROWS * CX * 2,
        moved=4000000,
    )(smooth, control.reshape(flat), rate_y.reshape(1, CY), vert)
    for part, band, dtype in ((0, inner, F32), (1, outer, BF16)):
        total = call(
            functools.partial(band_kernel, part),
            struct(flat, dtype),
            [VMEM] * 3,
            flops=2 * 2 * ROWS * ROWS * CX,
            moved=2000000,
        )(total, band.reshape(flat), y_weights)
    return total.reshape(shape)


def solution(mesh):
    placed = (
        P(None, None, "ry", "rx"),
        P(None, None, "ry", "rx"),
        P(("ry", "rx"), None),
        P(("ry", "rx")),
        P(None, ("ry", "rx")),
        P(("ry", "rx")),
        P(),
        P("ry"),
        P(),
    )
    return jax.shard_map(
        body, mesh=mesh, in_specs=placed, out_specs=P(None, None, "ry", "rx"), check_vma=False
    )
```

```python
import functools

import jax
import jax.numpy as jnp
from jax import lax
from jax.experimental import pallas as pl
from jax.experimental.pallas import tpu as pltpu
from jax.sharding import PartitionSpec as P

LEV = 64
CY = 8
CX = 128
SLOTS = 1024
ROWS = LEV * CY
TILES = 16
PARTS = SLOTS // CX
VMEM = pl.BlockSpec(memory_space=pltpu.VMEM)
HBM = pl.BlockSpec(memory_space=pltpu.HBM)
F32 = jnp.float32
BF16 = jnp.bfloat16
I32 = jnp.int32
ACROSS = (((1,), (1,)), ((), ()))


def iota(shape, axis):
    return lax.broadcasted_iota(I32, shape, axis)


def pack_kernel(
    count_ref, tile_hbm, cell_hbm, value_hbm, out_ref, tiles, cells, values, sems
):
    pairs = ((tile_hbm, tiles), (cell_hbm, cells), (value_hbm, values))
    copies = [pltpu.make_async_copy(a, b, sems.at[i]) for i, (a, b) in enumerate(pairs)]
    for copy in copies:
        copy.start()
    before = (iota((CX, CX), 0) <= iota((CX, CX), 1)).astype(F32)
    before = jnp.concatenate([before, jnp.ones((CX, CX), F32)], axis=0).astype(BF16)
    above = (iota((CX, CX), 0) > iota((CX, CX), 1)).astype(F32).astype(BF16)
    slot = iota((PARTS, CX), 0) * CX + iota((PARTS, CX), 1)
    for copy in copies:
        copy.wait()
    used = slot < count_ref[0]
    tile = jnp.where(used, tiles[...], -1)
    cell = cells[...]
    fields = [
        (cell // CX - ROWS // 2).astype(F32),
        (tile + 1).astype(F32),
        (cell % CX - CX // 2).astype(F32),
        values[0:1].reshape(PARTS, CX),
        values[1:2].reshape(PARTS, CX),
    ]

    named = jnp.concatenate([jnp.where(tile == t, 1.0, 0.0) for t in range(TILES)], axis=0)
    both = named.astype(BF16)
    lower = jnp.dot(above, both, preferred_element_type=F32).astype(BF16)
    rank = jnp.dot(jnp.concatenate([both, lower], axis=1), before, preferred_element_type=F32)
    rank = jnp.sum((named * (rank - 1.0)).reshape(TILES, PARTS, CX), axis=0)
    rank = jnp.where(used, rank, float(SLOTS)).astype(I32)

    row, lane = rank // CX, rank % CX
    picked, lanes = [], []
    for part in range(PARTS):
        here = iota((PARTS, CX), 0) == row[part : part + 1]
        rows = [jnp.where(here, field[part : part + 1], 0.0) for field in fields]
        picked.append(jnp.concatenate(rows, axis=0).astype(BF16))
        lanes.append(jnp.where(iota((CX, CX), 0) == lane[part : part + 1], 1.0, 0.0).astype(BF16))
    ordered = lax.dot_general(
        jnp.concatenate(picked, axis=1), jnp.concatenate(lanes, axis=1), ACROSS, preferred_element_type=F32
    )
    place, named, column, first, second = (ordered[i * PARTS : (i + 1) * PARTS] for i in range(5))
    column = jnp.where(named > 0.0, (named - 1.0) * CX + column, 4.0 * TILES * CX)
    for t in range(TILES):
        out_ref[t] = jnp.concatenate([place, column - t * CX, first, second], axis=0).astype(BF16)


def lon_kernel(
    record_ref, own_hbm, rate_x_hbm, sum_ref, x_ref, own_ref, rate_x_ref, rate_ref, list_ref, sems
):
    copies = [
        pltpu.make_async_copy(rate_x_hbm, rate_x_ref, sems.at[0]),
        pltpu.make_async_copy(own_hbm, own_ref, sems.at[1]),
    ]
    for copy in copies:
        copy.start()

    rows = TILES * PARTS
    record = record_ref[...].astype(F32)
    field = lambda f: record[:, f * PARTS : (f + 1) * PARTS, :].reshape(rows, CX)
    column = field(1)
    reached = jnp.logical_and(column >= -1.5 * CX, column < 1.5 * CX)
    some = jnp.max(jnp.where(reached, 1.0, 0.0), axis=1, keepdims=True)
    some = jnp.broadcast_to(some, (rows, CX)).astype(BF16)
    across = (((0,), (0,)), ((), ()))
    upto = (iota((rows, rows), 0) <= iota((rows, rows), 1)).astype(F32).astype(BF16)
    under = (iota((rows, rows), 0) < iota((rows, rows), 1)).astype(F32).astype(BF16)
    upto = lax.dot_general(some, upto, across, preferred_element_type=F32)
    under = lax.dot_general(some, under, across, preferred_element_type=F32)
    target_row = iota((rows, rows), 0).astype(F32)
    moved = jnp.logical_and(under == target_row, upto == target_row + 1.0)
    moved = jnp.where(moved, 1.0, 0.0).astype(BF16)
    for f in range(4):
        list_ref[f] = jnp.dot(moved, field(f).astype(BF16), preferred_element_type=F32)
    used_rows = jnp.max(upto).astype(I32)

    tile, tiles = lax.axis_index("rx"), lax.axis_size("rx")
    copies[0].wait()
    rates = rate_x_ref[pl.ds(tile, 1), :]
    source = iota((CX, CX), 0)
    target = iota((CX, CX), 1)
    weights = []
    for part in range(3):
        far = jnp.abs(source + (part - 1) * CX - target)
        near = far <= CX
        if part == 0:
            near = jnp.logical_and(near, tile > 0)
        if part == 2:
            near = jnp.logical_and(near, tile < tiles - 1)
        weights.append(jnp.where(near, jnp.exp(-far.astype(F32) * rates / CX), 0.0))
    even = tile % 2 == 0
    x_ref[0:CX] = jnp.where(even, weights[2], weights[0]).astype(BF16)
    x_ref[CX : 2 * CX] = jnp.where(even, weights[0], weights[2]).astype(BF16)
    middle = weights[1].astype(BF16)
    rate_ref[...] = jnp.broadcast_to(rates * (-1.0 / CX), (CX, CX)).T
    copies[1].wait()
    for c in range(2):
        sum_ref[:, c * CX : (c + 1) * CX] = jnp.dot(
            own_ref[c * ROWS : (c + 1) * ROWS], middle, preferred_element_type=F32
        )

    def add(start):
        record = list_ref[:, pl.ds(pl.multiple_of(start, PARTS), PARTS), :]
        places = iota((ROWS, CX), 0) - ROWS // 2
        columns = (iota((CX, CX), 0) - CX // 2).astype(F32)
        hits, spreads = [], []
        for part in range(PARTS):
            place, column, first, second = (record[f, part : part + 1] for f in range(4))
            hits.append(jnp.where(places == place.astype(I32), 1.0, 0.0).astype(BF16))
            far = jnp.abs(columns - column)
            weight = jnp.where(far <= CX, jnp.exp(far * rate_ref[...]), 0.0)
            spreads.append(jnp.concatenate([weight * first, weight * second], axis=0).astype(BF16))
        sum_ref[...] += lax.dot_general(
            jnp.concatenate(hits, axis=1), jnp.concatenate(spreads, axis=1), ACROSS, preferred_element_type=F32
        )

    def step(i, carry):
        add(2 * PARTS * i)
        add(2 * PARTS * i + PARTS)
        return carry

    lax.fori_loop(0, (used_rows + 2 * PARTS - 1) // (2 * PARTS), step, 0)


def dense_kernel(sum_ref, near_ref, far_ref, x_ref, out_ref):
    for c in range(2):
        at = slice(c * ROWS, (c + 1) * ROWS)
        total = sum_ref[:, c * CX : (c + 1) * CX]
        total += jnp.dot(near_ref[at], x_ref[0:CX], preferred_element_type=F32)
        total += jnp.dot(far_ref[at], x_ref[CX : 2 * CX], preferred_element_type=F32)
        out_ref[at] = total.astype(BF16)


def own_kernel(smooth_ref, control_ref, rate_y_ref, vert_ref, total_ref, y_ref):
    band, bands = lax.axis_index("ry"), lax.axis_size("ry")
    row = iota((CY, CX), 0)
    other = iota((CY, CX), 1) % CY
    rate = jnp.zeros((CY, CX), F32)
    for y in range(CY):
        rate = jnp.where(row == y, rate_y_ref[0:1, y : y + 1], rate)
    spread = (iota((ROWS, LEV), 0) // CY == iota((ROWS, LEV), 1)).astype(BF16)
    weights = []
    for part in range(3):
        far = jnp.abs(other + (part - 1) * CY - row)
        near = far <= CY
        if part == 0:
            near = jnp.logical_and(near, band > 0)
        if part == 2:
            near = jnp.logical_and(near, band < bands - 1)
        weight = jnp.where(near, jnp.exp(-far.astype(F32) * rate / CY), 0.0)
        weights.append(jnp.concatenate([weight.astype(BF16).astype(F32)] * (ROWS // CX), axis=1))
    even = band % 2 == 0
    weights = [jnp.where(even, weights[2], weights[0]), weights[1], jnp.where(even, weights[0], weights[2])]
    for c in range(2):
        at = slice(c * ROWS, (c + 1) * ROWS)
        tall = jnp.dot(spread, vert_ref[c], preferred_element_type=F32).astype(BF16)
        wide = lax.dot_general(tall, spread, ACROSS, preferred_element_type=F32).reshape(LEV, CY, ROWS)
        for part in (0, 2):
            product = (wide * weights[part][None]).reshape(ROWS, ROWS)
            y_ref[part // 2, c] = product.astype(BF16)
        middle = (wide * weights[1][None]).reshape(ROWS, ROWS).astype(BF16)
        mixed = jnp.dot(middle, smooth_ref[at], preferred_element_type=F32)
        total_ref[at] = control_ref[at].astype(F32) + mixed


def band_kernel(part, total_ref, band_ref, y_ref, out_ref):
    for c in range(2):
        at = slice(c * ROWS, (c + 1) * ROWS)
        mixed = jnp.dot(y_ref[part, c], band_ref[at], preferred_element_type=F32)
        out_ref[at] = (total_ref[at] + mixed).astype(out_ref.dtype)


def call(kernel, out_shape, specs, scratch=(), flops=0, moved=0):
    many = isinstance(out_shape, (list, tuple))
    return pl.pallas_call(
        kernel,
        out_shape=out_shape,
        in_specs=specs,
        out_specs=[VMEM] * len(out_shape) if many else VMEM,
        scratch_shapes=list(scratch),
        cost_estimate=pl.CostEstimate(flops=flops, bytes_accessed=moved, transcendentals=0),
        compiler_params=pltpu.CompilerParams(vmem_limit_bytes=24 * 2**20),
    )


def body(control, forcing, obs_tile, obs_cell, obs_value, obs_count, rate_x, rate_y, vert):
    shape = control.shape
    flat = (2 * ROWS, CX)
    bands, tiles = lax.axis_size("ry"), lax.axis_size("rx")
    struct = jax.ShapeDtypeStruct

    inputs = (obs_count, obs_tile.reshape(PARTS, CX), obs_cell.reshape(PARTS, CX), obs_value)
    packed = call(
        pack_kernel,
        struct((TILES, 4 * PARTS, CX), BF16),
        [pl.BlockSpec(memory_space=pltpu.SMEM)] + [HBM] * 3,
        [
            pltpu.VMEM((PARTS, CX), I32),
            pltpu.VMEM((PARTS, CX), I32),
            pltpu.VMEM((2, SLOTS), F32),
            pltpu.SemaphoreType.DMA((3,)),
        ],
        flops=3 * 10**9,
        moved=200000,
    )(inputs[0], *(pltpu.with_memory_space_constraint(x, pltpu.HBM) for x in inputs[1:]))
    records = lax.all_to_all(packed, "rx", 0, 0, tiled=True)

    held, _ = lax.optimization_barrier((forcing, packed))
    inner = lax.ppermute(held, "rx", [(i, i ^ 1) for i in range(tiles)])
    outer = lax.ppermute(held, "rx", [(i, ((i + 1) ^ 1) - 1) for i in range(1, tiles - 1)])

    total, x_weights = call(
        lon_kernel,
        [struct((ROWS, 2 * CX), F32), struct((2 * CX, CX), BF16)],
        [VMEM, HBM, HBM],
        [
            pltpu.VMEM(flat, BF16),
            pltpu.VMEM((TILES, CX), F32),
            pltpu.VMEM((CX, CX), F32),
            pltpu.VMEM((4, TILES * PARTS, CX), F32),
            pltpu.SemaphoreType.DMA((2,)),
        ],
        flops=2 * ROWS * 256 * TILES * SLOTS,
        moved=1000000,
    )(records, forcing.reshape(flat), rate_x.reshape(TILES, CX))

    smooth = call(dense_kernel, struct(flat, BF16), [VMEM] * 4, flops=2 * 1024 * 256 * 128, moved=1000000)(
        total, inner.reshape(flat), outer.reshape(flat), x_weights
    )
    wide = smooth.reshape(shape)
    inner = lax.ppermute(wide, "ry", [(i, i ^ 1) for i in range(bands)])
    outer = lax.ppermute(wide, "ry", [(i, ((i + 1) ^ 1) - 1) for i in range(1, bands - 1)])
    total, y_weights = call(
        own_kernel,
        [struct(flat, F32), struct((2, 2, ROWS, ROWS), BF16)],
        [VMEM] * 4,
        flops=2 * 2 * ROWS * ROWS * CX * 2,
        moved=4000000,
    )(smooth, control.reshape(flat), rate_y.reshape(1, CY), vert)
    for part, band, dtype in ((0, inner, F32), (1, outer, BF16)):
        total = call(
            functools.partial(band_kernel, part),
            struct(flat, dtype),
            [VMEM] * 3,
            flops=2 * 2 * ROWS * ROWS * CX,
            moved=2000000,
        )(total, band.reshape(flat), y_weights)
    return total.reshape(shape)


def solution(mesh):
    placed = (
        P(None, None, "ry", "rx"),
        P(None, None, "ry", "rx"),
        P(("ry", "rx"), None),
        P(("ry", "rx")),
        P(None, ("ry", "rx")),
        P(("ry", "rx")),
        P(),
        P("ry"),
        P(),
    )
    return jax.shard_map(
        body, mesh=mesh, in_specs=placed, out_specs=P(None, None, "ry", "rx"), check_vma=False
    )
```

```python
import functools

import jax
import jax.numpy as jnp
from jax import lax
from jax.experimental import pallas as pl
from jax.experimental.pallas import tpu as pltpu
from jax.sharding import PartitionSpec as P

LEV = 64
CY = 8
CX = 128
SLOTS = 1024
ROWS = LEV * CY
TILES = 16
PARTS = SLOTS // CX
VMEM = pl.BlockSpec(memory_space=pltpu.VMEM)
HBM = pl.BlockSpec(memory_space=pltpu.HBM)
F32 = jnp.float32
BF16 = jnp.bfloat16
I32 = jnp.int32
ACROSS = (((1,), (1,)), ((), ()))


def iota(shape, axis):
    return lax.broadcasted_iota(I32, shape, axis)


def pack_kernel(
    count_ref, tile_hbm, cell_hbm, value_hbm, out_ref, tiles, cells, values, sems
):
    pairs = ((tile_hbm, tiles), (cell_hbm, cells), (value_hbm, values))
    copies = [pltpu.make_async_copy(a, b, sems.at[i]) for i, (a, b) in enumerate(pairs)]
    for copy in copies:
        copy.start()
    before = (iota((CX, CX), 0) <= iota((CX, CX), 1)).astype(F32)
    before = jnp.concatenate([before, jnp.ones((CX, CX), F32)], axis=0).astype(BF16)
    above = (iota((CX, CX), 0) > iota((CX, CX), 1)).astype(F32).astype(BF16)
    slot = iota((PARTS, CX), 0) * CX + iota((PARTS, CX), 1)
    for copy in copies:
        copy.wait()
    used = slot < count_ref[0]
    tile = jnp.where(used, tiles[...], -1)
    cell = cells[...]
    fields = [
        (cell // CX - ROWS // 2).astype(F32),
        (tile + 1).astype(F32),
        (cell % CX - CX // 2).astype(F32),
        values[0:1].reshape(PARTS, CX),
        values[1:2].reshape(PARTS, CX),
    ]

    named = jnp.concatenate([jnp.where(tile == t, 1.0, 0.0) for t in range(TILES)], axis=0)
    both = named.astype(BF16)
    lower = jnp.dot(above, both, preferred_element_type=F32).astype(BF16)
    rank = jnp.dot(jnp.concatenate([both, lower], axis=1), before, preferred_element_type=F32)
    rank = jnp.sum((named * (rank - 1.0)).reshape(TILES, PARTS, CX), axis=0)
    rank = jnp.where(used, rank, float(SLOTS)).astype(I32)

    row, lane = rank // CX, rank % CX
    picked, lanes = [], []
    for part in range(PARTS):
        here = iota((PARTS, CX), 0) == row[part : part + 1]
        rows = [jnp.where(here, field[part : part + 1], 0.0) for field in fields]
        picked.append(jnp.concatenate(rows, axis=0).astype(BF16))
        lanes.append(jnp.where(iota((CX, CX), 0) == lane[part : part + 1], 1.0, 0.0).astype(BF16))
    ordered = lax.dot_general(
        jnp.concatenate(picked, axis=1), jnp.concatenate(lanes, axis=1), ACROSS, preferred_element_type=F32
    )
    place, named, column, first, second = (ordered[i * PARTS : (i + 1) * PARTS] for i in range(5))
    column = jnp.where(named > 0.0, (named - 1.0) * CX + column, 4.0 * TILES * CX)
    for t in range(TILES):
        out_ref[t] = jnp.concatenate([place, column - t * CX, first, second], axis=0).astype(BF16)


def lon_kernel(
    record_ref, own_hbm, rate_x_hbm, sum_ref, x_ref, own_ref, rate_x_ref, rate_ref, list_ref, sems
):
    copies = [
        pltpu.make_async_copy(rate_x_hbm, rate_x_ref, sems.at[0]),
        pltpu.make_async_copy(own_hbm, own_ref, sems.at[1]),
    ]
    for copy in copies:
        copy.start()

    rows = TILES * PARTS
    record = record_ref[...].astype(F32)
    field = lambda f: record[:, f * PARTS : (f + 1) * PARTS, :].reshape(rows, CX)
    column = field(1)
    reached = jnp.logical_and(column >= -1.5 * CX, column < 1.5 * CX)
    count = jnp.sum(jnp.where(reached, 1.0, 0.0), axis=1, keepdims=True)
    count = jnp.broadcast_to(count, (rows, CX))
    some = jnp.where(count > 0.0, 1.0, 0.0).astype(BF16)
    count = count.astype(BF16)
    row, other = iota((rows, rows), 0), iota((rows, rows), 1)
    source = row // PARTS == other // PARTS
    matrix = lambda mask: mask.astype(F32).astype(BF16)
    turned = lambda x, mask: lax.dot_general(x, matrix(mask), (((0,), (0,)), ((), ())), preferred_element_type=F32)
    flag = turned(some, row == other)
    following = turned(some, jnp.logical_and(row == other + 1, source))
    span = turned(some, source)
    within = turned(count, source)
    fits = jnp.logical_and(span > 1.0, within <= CX * (span - 1.0))
    merged = jnp.where(fits, flag * (1.0 - following), 0.0)
    kept = flag - merged
    ahead = jnp.dot(kept.astype(BF16), matrix(row < other), preferred_element_type=F32)
    place = ahead - merged * (span - 1.0)
    moved = matrix(jnp.logical_and(flag > 0.0, place == row.astype(F32)))
    for f in range(4):
        kept_slots = jnp.where(reached, field(f), 0.0).astype(BF16)
        list_ref[f] = jnp.dot(moved, kept_slots, preferred_element_type=F32)
    used_rows = jnp.max(ahead + kept).astype(I32)

    tile, tiles = lax.axis_index("rx"), lax.axis_size("rx")
    copies[0].wait()
    rates = rate_x_ref[pl.ds(tile, 1), :]
    source = iota((CX, CX), 0)
    target = iota((CX, CX), 1)
    weights = []
    for part in range(3):
        far = jnp.abs(source + (part - 1) * CX - target)
        near = far <= CX
        if part == 0:
            near = jnp.logical_and(near, tile > 0)
        if part == 2:
            near = jnp.logical_and(near, tile < tiles - 1)
        weights.append(jnp.where(near, jnp.exp(-far.astype(F32) * rates / CX), 0.0))
    even = tile % 2 == 0
    x_ref[0:CX] = jnp.where(even, weights[2], weights[0]).astype(BF16)
    x_ref[CX : 2 * CX] = jnp.where(even, weights[0], weights[2]).astype(BF16)
    middle = weights[1].astype(BF16)
    rate_ref[...] = jnp.broadcast_to(rates * (-1.0 / CX), (CX, CX)).T
    copies[1].wait()
    for c in range(2):
        sum_ref[:, c * CX : (c + 1) * CX] = jnp.dot(
            own_ref[c * ROWS : (c + 1) * ROWS], middle, preferred_element_type=F32
        )

    def add(start):
        record = list_ref[:, pl.ds(pl.multiple_of(start, PARTS), PARTS), :]
        places = iota((ROWS, CX), 0) - ROWS // 2
        columns = (iota((CX, CX), 0) - CX // 2).astype(F32)
        hits, spreads = [], []
        for part in range(PARTS):
            place, column, first, second = (record[f, part : part + 1] for f in range(4))
            hits.append(jnp.where(places == place.astype(I32), 1.0, 0.0).astype(BF16))
            far = jnp.abs(columns - column)
            weight = jnp.where(far <= CX, jnp.exp(far * rate_ref[...]), 0.0)
            spreads.append(jnp.concatenate([weight * first, weight * second], axis=0).astype(BF16))
        sum_ref[...] += lax.dot_general(
            jnp.concatenate(hits, axis=1), jnp.concatenate(spreads, axis=1), ACROSS, preferred_element_type=F32
        )

    def step(i, carry):
        add(2 * PARTS * i)
        add(2 * PARTS * i + PARTS)
        return carry

    lax.fori_loop(0, (used_rows + 2 * PARTS - 1) // (2 * PARTS), step, 0)


def dense_kernel(sum_ref, near_ref, far_ref, x_ref, out_ref):
    for c in range(2):
        at = slice(c * ROWS, (c + 1) * ROWS)
        total = sum_ref[:, c * CX : (c + 1) * CX]
        total += jnp.dot(near_ref[at], x_ref[0:CX], preferred_element_type=F32)
        total += jnp.dot(far_ref[at], x_ref[CX : 2 * CX], preferred_element_type=F32)
        out_ref[at] = total.astype(BF16)


def own_kernel(smooth_ref, control_ref, rate_y_ref, vert_ref, total_ref, y_ref):
    band, bands = lax.axis_index("ry"), lax.axis_size("ry")
    row = iota((CY, CX), 0)
    other = iota((CY, CX), 1) % CY
    rate = jnp.zeros((CY, CX), F32)
    for y in range(CY):
        rate = jnp.where(row == y, rate_y_ref[0:1, y : y + 1], rate)
    spread = (iota((ROWS, LEV), 0) // CY == iota((ROWS, LEV), 1)).astype(BF16)
    weights = []
    for part in range(3):
        far = jnp.abs(other + (part - 1) * CY - row)
        near = far <= CY
        if part == 0:
            near = jnp.logical_and(near, band > 0)
        if part == 2:
            near = jnp.logical_and(near, band < bands - 1)
        weight = jnp.where(near, jnp.exp(-far.astype(F32) * rate / CY), 0.0)
        weights.append(jnp.concatenate([weight.astype(BF16).astype(F32)] * (ROWS // CX), axis=1))
    even = band % 2 == 0
    weights = [jnp.where(even, weights[2], weights[0]), weights[1], jnp.where(even, weights[0], weights[2])]
    for c in range(2):
        at = slice(c * ROWS, (c + 1) * ROWS)
        tall = jnp.dot(spread, vert_ref[c], preferred_element_type=F32).astype(BF16)
        wide = lax.dot_general(tall, spread, ACROSS, preferred_element_type=F32).reshape(LEV, CY, ROWS)
        for part in (0, 2):
            product = (wide * weights[part][None]).reshape(ROWS, ROWS)
            y_ref[part // 2, c] = product.astype(BF16)
        middle = (wide * weights[1][None]).reshape(ROWS, ROWS).astype(BF16)
        mixed = jnp.dot(middle, smooth_ref[at], preferred_element_type=F32)
        total_ref[at] = control_ref[at].astype(F32) + mixed


def band_kernel(part, total_ref, band_ref, y_ref, out_ref):
    for c in range(2):
        at = slice(c * ROWS, (c + 1) * ROWS)
        mixed = jnp.dot(y_ref[part, c], band_ref[at], preferred_element_type=F32)
        out_ref[at] = (total_ref[at] + mixed).astype(out_ref.dtype)


def call(kernel, out_shape, specs, scratch=(), flops=0, moved=0):
    many = isinstance(out_shape, (list, tuple))
    return pl.pallas_call(
        kernel,
        out_shape=out_shape,
        in_specs=specs,
        out_specs=[VMEM] * len(out_shape) if many else VMEM,
        scratch_shapes=list(scratch),
        cost_estimate=pl.CostEstimate(flops=flops, bytes_accessed=moved, transcendentals=0),
        compiler_params=pltpu.CompilerParams(vmem_limit_bytes=24 * 2**20),
    )


def body(control, forcing, obs_tile, obs_cell, obs_value, obs_count, rate_x, rate_y, vert):
    shape = control.shape
    flat = (2 * ROWS, CX)
    bands, tiles = lax.axis_size("ry"), lax.axis_size("rx")
    struct = jax.ShapeDtypeStruct

    inputs = (obs_count, obs_tile.reshape(PARTS, CX), obs_cell.reshape(PARTS, CX), obs_value)
    packed = call(
        pack_kernel,
        struct((TILES, 4 * PARTS, CX), BF16),
        [pl.BlockSpec(memory_space=pltpu.SMEM)] + [HBM] * 3,
        [
            pltpu.VMEM((PARTS, CX), I32),
            pltpu.VMEM((PARTS, CX), I32),
            pltpu.VMEM((2, SLOTS), F32),
            pltpu.SemaphoreType.DMA((3,)),
        ],
        flops=3 * 10**9,
        moved=200000,
    )(inputs[0], *(pltpu.with_memory_space_constraint(x, pltpu.HBM) for x in inputs[1:]))
    records = lax.all_to_all(packed, "rx", 0, 0, tiled=True)

    held, _ = lax.optimization_barrier((forcing, packed))
    inner = lax.ppermute(held, "rx", [(i, i ^ 1) for i in range(tiles)])
    outer = lax.ppermute(held, "rx", [(i, ((i + 1) ^ 1) - 1) for i in range(1, tiles - 1)])

    total, x_weights = call(
        lon_kernel,
        [struct((ROWS, 2 * CX), F32), struct((2 * CX, CX), BF16)],
        [VMEM, HBM, HBM],
        [
            pltpu.VMEM(flat, BF16),
            pltpu.VMEM((TILES, CX), F32),
            pltpu.VMEM((CX, CX), F32),
            pltpu.VMEM((4, TILES * PARTS, CX), F32),
            pltpu.SemaphoreType.DMA((2,)),
        ],
        flops=2 * ROWS * 256 * TILES * SLOTS,
        moved=1000000,
    )(records, forcing.reshape(flat), rate_x.reshape(TILES, CX))

    smooth = call(dense_kernel, struct(flat, BF16), [VMEM] * 4, flops=2 * 1024 * 256 * 128, moved=1000000)(
        total, inner.reshape(flat), outer.reshape(flat), x_weights
    )
    wide = smooth.reshape(shape)
    inner = lax.ppermute(wide, "ry", [(i, i ^ 1) for i in range(bands)])
    outer = lax.ppermute(wide, "ry", [(i, ((i + 1) ^ 1) - 1) for i in range(1, bands - 1)])
    total, y_weights = call(
        own_kernel,
        [struct(flat, F32), struct((2, 2, ROWS, ROWS), BF16)],
        [VMEM] * 4,
        flops=2 * 2 * ROWS * ROWS * CX * 2,
        moved=4000000,
    )(smooth, control.reshape(flat), rate_y.reshape(1, CY), vert)
    for part, band, dtype in ((0, inner, F32), (1, outer, BF16)):
        total = call(
            functools.partial(band_kernel, part),
            struct(flat, dtype),
            [VMEM] * 3,
            flops=2 * 2 * ROWS * ROWS * CX,
            moved=2000000,
        )(total, band.reshape(flat), y_weights)
    return total.reshape(shape)


def solution(mesh):
    placed = (
        P(None, None, "ry", "rx"),
        P(None, None, "ry", "rx"),
        P(("ry", "rx"), None),
        P(("ry", "rx")),
        P(None, ("ry", "rx")),
        P(("ry", "rx")),
        P(),
        P("ry"),
        P(),
    )
    return jax.shard_map(
        body, mesh=mesh, in_specs=placed, out_specs=P(None, None, "ry", "rx"), check_vma=False
    )
```
